32 devices in a mesh: row: 8 (over y, x, core), col: 4 (over z).
Axes of the slice: x: 2, y: 2, z: 4, core: 2. Of those that a mesh axis runs over, the one named last changes fastest.
Arguments:
- covariance: bfloat16 [16384, 16384], P('row', 'col'), as said below
- coef_index: int32 [3, 16384], replicated, may hold values from 0 to 127, as said below
Outputs:
- grid_cov: float32 [4608, 4608], P('row', 'col')
The draws below stay inside these ranges and needn't reach their ends.
Inputs may be any that keep to these rules, and one draw needn't show every extreme that they name: `coef_index`: every (degree l, order m, parity c) with m <= l < 128, c in 0 and 1, and c = 0 where m = 0, names exactly one row. The rows of each order are consecutive: cosine terms by rising degree, then sine terms by rising degree. Orders m and 128 - m (0 and 64) stand next to each other, the smaller first, and fill 2 * 128 rows together; pairs start at multiples of 256. Columns follow the same index. `covariance`: Symmetric.
All inputs are finite; a program needn't handle non-finite values.
Results may differ from the reference program's by a relative error of at most 0.0028.
Values sent between devices are 32-bit elements; how exact they have to be, the bound alone decides.
No kernel may reach another device: no remote copies, remote signals or barrier semaphores. Data moves between devices by JAX's collectives and lax.ppermute only.
A program may use at most 128 MiB of HBM per device.

```python
import math
import jax
import jax.numpy as jnp
from jax import lax

LL = 128
NLON = 384
NLAT = 12
K = 16384
NPTS = 4608


def draw_covariance(key, part):
    key_scale = jax.random.fold_in(key, 11)
    key_diag = jax.random.fold_in(key, 12)
    key_noise = jax.random.fold_in(key, 13)
    scales = jnp.exp(jax.random.uniform(key_scale, (K,), jnp.float32, 0.0, math.log(10.0)))
    diag_vals = jax.random.uniform(key_diag, (K,), jnp.float32, 0.5, 1.5)
    block_width = min(1024, K)
    nblocks = K // block_width

    def one_row(row_block):

        def one_tile(col_block):
            lower = jnp.minimum(row_block, col_block)
            upper = jnp.maximum(row_block, col_block)
            tile_key = jax.random.fold_in(key_noise, lower * nblocks + upper)
            noise = jax.random.normal(tile_key, (block_width, block_width), jnp.float32)
            flipped = jnp.where(row_block > col_block, noise.T, noise)
            return jnp.where(row_block == col_block, (noise + noise.T) * 0.70710678, flipped)
        tiles = jax.vmap(one_tile)(jnp.arange(nblocks, dtype=jnp.int32))
        tiles = jnp.transpose(tiles, (1, 0, 2)).reshape(block_width, K)
        row_scale = lax.dynamic_slice_in_dim(scales, row_block * block_width, block_width)
        row_diag = lax.dynamic_slice_in_dim(diag_vals, row_block * block_width, block_width)
        on_diag = (row_block * block_width + jnp.arange(block_width, dtype=jnp.int32))[:, None] == jnp.arange(K, dtype=jnp.int32)[None, :]
        entry = row_scale[:, None] * scales[None, :] * (0.5 * tiles + jnp.where(on_diag, row_diag[:, None], 0.0)) / (8.0 * K)
        return entry.astype(jnp.bfloat16)
    rows_out = lax.map(one_row, jnp.arange(nblocks, dtype=jnp.int32))
    return rows_out.reshape(K, K)


def draw_coef_index(key, part):
    pair_order = jax.random.permutation(jax.random.fold_in(key, 21), LL // 2).astype(jnp.int32)
    row_ids = jnp.arange(K, dtype=jnp.int32)
    pair_slot = row_ids // (2 * LL)
    offset = row_ids % (2 * LL)
    pair_ids = pair_order[pair_slot]
    first_order = pair_ids
    second_order = jnp.where(pair_ids == 0, LL // 2, LL - pair_ids)
    first_size = jnp.where(pair_ids == 0, LL, 2 * (LL - pair_ids))
    in_first = offset < first_size
    order_ids = jnp.where(in_first, first_order, second_order)
    within = jnp.where(in_first, offset, offset - first_size)
    order_len = LL - order_ids
    parity = jnp.where(order_ids == 0, 0, (within >= order_len).astype(jnp.int32))
    degree = order_ids + within - parity * order_len
    return jnp.stack([degree, order_ids, parity]).astype(jnp.int32)


def setup_inputs(seed: int = 0) -> dict:
    splits = jax.random.split(jax.random.key(seed), 3)
    return {
        "covariance": draw_covariance(jax.random.fold_in(splits[2], 71), 0),
        "coef_index": draw_coef_index(jax.random.fold_in(splits[2], 71), 0),
    }


def legendre_rows(lat_count, lon_count, degree_count):
    grid_rows = lon_count // 2
    first_row = grid_rows // 2 - lat_count // 2
    colatitude = (first_row + jnp.arange(lat_count, dtype=jnp.float32) + 0.5) * (math.pi / grid_rows)
    cosine = jnp.cos(colatitude)[:, None]
    sine_vals = jnp.sin(colatitude)[:, None]
    orders = jnp.arange(degree_count, dtype=jnp.float32)[None, :]
    growth = jnp.sqrt((2.0 * orders + 1.0) / jnp.maximum(2.0 * orders, 1.0))
    growth = jnp.where(orders == 1.0, jnp.sqrt(jnp.float32(3.0)), jnp.where(orders == 0.0, 1.0, growth))
    sectoral = jnp.exp(jnp.cumsum(jnp.log(growth), axis=1) + orders * jnp.log(sine_vals))

    def advance(state_pair, degree):
        before, earlier = state_pair
        deg_sum = degree + orders
        deg_diff = degree - orders
        alpha_lm = jnp.sqrt(jnp.maximum((2.0 * degree - 1.0) * (2.0 * degree + 1.0), 0.0) / jnp.maximum(deg_diff * deg_sum, 1.0))
        beta_lm = jnp.sqrt(jnp.maximum((2.0 * degree + 1.0) * (deg_sum - 1.0) * (deg_diff - 1.0), 0.0) / jnp.maximum(deg_diff * deg_sum * (2.0 * degree - 3.0), 1.0))
        general = alpha_lm * cosine * before - beta_lm * earlier
        current = jnp.where(orders < degree, general, jnp.where(orders == degree, sectoral, 0.0))
        return ((current, before), current)
    start_pair = (jnp.zeros((lat_count, degree_count), jnp.float32), jnp.zeros((lat_count, degree_count), jnp.float32))
    _, stacked = lax.scan(advance, start_pair, jnp.arange(degree_count, dtype=jnp.float32), unroll=16)
    return jnp.transpose(stacked, (1, 0, 2)).reshape(lat_count, degree_count * degree_count)

def fourier(modes, parity, longitudes):
    phases = longitudes[:, None] * modes[None, :] % NLON
    angles = phases.astype(jnp.float32) * (2.0 * math.pi / NLON)
    return jnp.where(parity[None, :] == 0, jnp.cos(angles), jnp.sin(angles))

def reference(covariance, coef_index):
    degree = coef_index[0]
    orders = coef_index[1]
    parity = coef_index[2]
    plm_table = legendre_rows(NLAT, NLON, LL)
    values = plm_table[:, degree * LL + orders]
    rounded = lax.optimization_barrier(values.astype(jnp.bfloat16)).astype(jnp.float32)
    rounded_t = rounded.T
    key_ids = 2 * orders + parity
    block_width = min(512, K)
    blocks = K // block_width

    def row_side(block_index):
        column_block = lax.dynamic_slice_in_dim(covariance, block_index * block_width, block_width, 1).astype(jnp.float32)
        product = rounded_t[:, :, None] * column_block[:, None, :]
        return jax.ops.segment_sum(product, key_ids, num_segments=2 * LL)
    row_pass = lax.map(row_side, jnp.arange(blocks, dtype=jnp.int32))
    row_pass_t = jnp.transpose(row_pass, (0, 3, 1, 2)).reshape(K, 2 * LL * NLAT)

    def col_side(latitude):
        weights = lax.dynamic_index_in_dim(values, latitude, 0, keepdims=False)
        return jax.ops.segment_sum(row_pass_t * weights[:, None], key_ids, num_segments=2 * LL)
    second = lax.map(col_side, jnp.arange(NLAT, dtype=jnp.int32))
    second = second.reshape(NLAT, 2 * LL, 2 * LL, NLAT)
    mode_ids = jnp.arange(2 * LL, dtype=jnp.int32)
    dft_table = fourier(mode_ids // 2, mode_ids % 2, jnp.arange(NLON, dtype=jnp.int32))
    half_done = jnp.einsum('akbi,jb->akji', second, dft_table, precision=lax.Precision.HIGHEST)
    grid_cov = jnp.einsum('akji,Jk->jiJa', half_done, dft_table, precision=lax.Precision.HIGHEST)
    return grid_cov.reshape(NPTS, NPTS)
```

```python
import functools
import math

import jax
import jax.numpy as jnp
from jax import lax
from jax.experimental import pallas as pl
from jax.experimental.pallas import tpu as pltpu
from jax.sharding import PartitionSpec as P

LL = 128
NLON = 384
NLAT = 12

F32 = jnp.float32
BF16 = jnp.bfloat16
ROWS16 = 16
CHIPS = 4
CHUNKS = NLAT // CHIPS
PAIR = 2 * LL
KEYS = 4
STEP = 2 * PAIR


def split(x):
    high = x.astype(BF16)
    return high, (x - high.astype(F32)).astype(BF16)


def dot3(a, b, dims):
    dg = functools.partial(
        lax.dot_general, dimension_numbers=(dims, ((), ())), preferred_element_type=F32
    )
    return dg(a[0], b[0]) + (dg(a[0], b[1]) + dg(a[1], b[0]))


def turn4(xs):
    lane = lax.broadcasted_iota(jnp.int32, xs[0].shape, 1)
    left = lane < 64
    even = (lane // 32) % 2 == 0
    out = [None] * 4
    halves = []
    for u in range(2):
        a, b = xs[u], xs[u + 2]
        halves.append(
            (jnp.where(left, a, pltpu.roll(b, 64, 1)), jnp.where(left, pltpu.roll(a, 64, 1), b))
        )
    for h in range(2):
        a, b = halves[0][h], halves[1][h]
        out[2 * h] = jnp.where(even, a, pltpu.roll(b, 32, 1))
        out[2 * h + 1] = jnp.where(even, pltpu.roll(a, 96, 1), b)
    return out


def legendre_table(by_degree, by_order):
    shape = (ROWS16, LL)
    lat = lax.broadcasted_iota(jnp.int32, shape, 0).astype(F32)
    colatitude = (NLON // 4 - NLAT // 2 + lat + 0.5) * (math.pi / (NLON // 2))
    cosine, sine = jnp.cos(colatitude), jnp.sin(colatitude)
    lane = lax.broadcasted_iota(jnp.int32, shape, 1)
    orders = lane.astype(F32)
    growth = jnp.sqrt((2.0 * orders + 1.0) / jnp.maximum(2.0 * orders, 1.0))
    growth = jnp.where(lane == 1, math.sqrt(3.0), jnp.where(lane == 0, 1.0, growth))
    total = jnp.log(growth)
    shift = 1
    while shift < LL:
        total = total + jnp.where(lane >= shift, pltpu.roll(total, shift, 1), 0.0)
        shift *= 2
    sectoral = jnp.exp(total + orders * jnp.log(sine))
    m8 = lax.broadcasted_iota(jnp.int32, (8, LL), 1).astype(F32)
    r8 = lax.broadcasted_iota(jnp.int32, (8, LL), 0)

    def block(b, carry):
        before, earlier = carry
        degree = (r8 + b * 8).astype(F32)
        plus, minus = degree + m8, degree - m8
        alpha = jnp.sqrt(
            jnp.maximum((2.0 * degree - 1.0) * (2.0 * degree + 1.0), 0.0)
            / jnp.maximum(minus * plus, 1.0)
        )
        beta = jnp.sqrt(
            jnp.maximum((2.0 * degree + 1.0) * (plus - 1.0) * (minus - 1.0), 0.0)
            / jnp.maximum(minus * plus * (2.0 * degree - 3.0), 1.0)
        )
        for r in range(8):
            l = b * 8 + r
            general = alpha[r : r + 1] * cosine * before - beta[r : r + 1] * earlier
            current = jnp.where(lane < l, general, jnp.where(lane == l, sectoral, 0.0))
            by_degree[pl.ds(pl.multiple_of(l * ROWS16, ROWS16), ROWS16), :] = current
            before, earlier = current, before
        return before, earlier

    zeros = jnp.zeros(shape, F32)
    lax.fori_loop(0, LL // 8, block, (zeros, zeros))
    for i in range(NLAT):
        by_order[pl.ds(i, LL, stride=ROWS16), :] = by_degree[pl.ds(i, LL, stride=ROWS16), :].T


def pair_weights(by_order, first, arrange):
    second = jnp.where(first == 0, LL // 2, LL - first)
    at = lambda m: arrange(by_order[pl.ds(pl.multiple_of(m * ROWS16, ROWS16), ROWS16), :])
    va, vb = at(first), at(second)
    na, nb = LL - first, LL - second
    lane = lax.broadcasted_iota(jnp.int32, va.shape, 1)
    wrap = lambda s: lax.bitwise_and(s, LL - 1)
    sines = pltpu.roll(va, wrap(2 * na), 1)
    real = first > 0
    begin = wrap(2 * na)
    return (
        (pltpu.roll(va, wrap(na), 1), None),
        (
            jnp.where((lane >= na) & real, sines, 0.0),
            jnp.where((lane < na) & real, sines, 0.0),
        ),
        (None, pltpu.roll(vb, wrap(nb + begin), 1)),
        (None, pltpu.roll(vb, wrap(2 * nb + begin), 1)),
    )


def order_sums_kernel(
    row_pairs, col_pairs, steps, orders, cov, *refs
):
    outs = refs[: CHUNKS * CHIPS]
    held, by_degree, by_order, row_w, row_wb, col_w, col_hi, col_lo, sems = refs[CHUNKS * CHIPS :]
    row_place, col_place = lax.axis_index("row"), lax.axis_index("col")
    chip = row_place // 2
    copy = lambda s: pltpu.make_async_copy(
        cov.at[:, pl.ds(pl.multiple_of(s * STEP, STEP), STEP)], held.at[s], sems.at[s]
    )
    for s in range(steps):
        copy(s).start()
    legendre_table(by_degree, by_order)
    row_w[...] = jnp.zeros_like(row_w)
    col_w[...] = jnp.zeros_like(col_w)

    def own_first(v):
        place = lax.broadcasted_iota(jnp.int32, v.shape, 0)
        for bit in (1, 2):
            up = pltpu.roll(v, ROWS16 - bit, 0)
            down = pltpu.roll(v, bit, 0)
            swapped = jnp.where(lax.bitwise_and(place, bit) == 0, up, down)
            v = jnp.where(lax.bitwise_and(chip, bit) == 0, v, swapped)
        return v

    for p in range(row_pairs):
        first = orders[row_place * row_pairs + p]
        for k, halves in enumerate(pair_weights(by_order, first, own_first)):
            for h, v in enumerate(halves):
                if v is not None:
                    row_w[2 * p + h, pl.ds(p * KEYS + k, NLAT, stride=row_pairs * KEYS), :] = v[
                        :NLAT
                    ]
    for h in range(2 * row_pairs):
        row_wb[:, h * LL : (h + 1) * LL] = row_w[h].astype(BF16)
    for p in range(col_pairs):
        first = orders[col_place * col_pairs + p]
        s, e = p // 2, p % 2
        for k, halves in enumerate(pair_weights(by_order, first, lambda v: v)):
            for h, v in enumerate(halves):
                if v is not None:
                    col_w[
                        2 * e + h,
                        pl.ds(s * NLAT * 2 * KEYS + e * KEYS + k, NLAT, stride=2 * KEYS),
                        :,
                    ] = v[:NLAT]
    for h in range(4):
        high, low = split(col_w[h])
        col_hi[:, h * LL : (h + 1) * LL] = high
        col_lo[:, h * LL : (h + 1) * LL] = low

    rows = NLAT * 2 * KEYS

    def step(s, carry):
        copy(s).wait()
        first = jnp.dot(row_wb[...], held[s], preferred_element_type=F32)
        own = pl.ds(pl.multiple_of(s * rows, rows), rows)
        second = dot3((col_hi[own, :], col_lo[own, :]), split(first), ((1,), (1,)))
        for t in range(CHUNKS):
            for g in range(NLAT // 4):
                parts = [
                    second[8 * (4 * g + u) : 8 * (4 * g + u + 1), LL * t : LL * (t + 1)]
                    for u in range(4)
                ]
                for d, part in enumerate(turn4(parts)):
                    outs[t * CHIPS + d][
                        pl.ds(pl.multiple_of(s * 8, 8), 8), pl.ds(g * LL, LL)
                    ] = part
        return carry

    lax.fori_loop(0, steps, step, 0)


def order_sums(covariance, orders):
    rows_dev, cols_dev = covariance.shape
    row_pairs, col_pairs, steps = rows_dev // PAIR, cols_dev // PAIR, cols_dev // STEP
    lanes = NLAT * row_pairs * KEYS
    out = jax.ShapeDtypeStruct((col_pairs * KEYS, lanes), F32)
    return pl.pallas_call(
        functools.partial(order_sums_kernel, row_pairs, col_pairs, steps),
        out_shape=[out] * (CHUNKS * CHIPS),
        in_specs=[pl.BlockSpec(memory_space=pltpu.SMEM), pl.BlockSpec(memory_space=pl.ANY)],
        out_specs=[pl.BlockSpec(memory_space=pltpu.VMEM)] * (CHUNKS * CHIPS),
        scratch_shapes=[
            pltpu.VMEM((steps, rows_dev, STEP), BF16),
            pltpu.VMEM((LL * ROWS16, LL), F32),
            pltpu.VMEM((LL * ROWS16, LL), F32),
            pltpu.VMEM((rows_dev // LL, lanes, LL), F32),
            pltpu.VMEM((lanes, rows_dev), BF16),
            pltpu.VMEM((STEP // LL, steps * NLAT * 2 * KEYS, LL), F32),
            pltpu.VMEM((steps * NLAT * 2 * KEYS, STEP), BF16),
            pltpu.VMEM((steps * NLAT * 2 * KEYS, STEP), BF16),
            pltpu.SemaphoreType.DMA((steps,)),
        ],
        compiler_params=pltpu.CompilerParams(vmem_limit_bytes=56 * 1024 * 1024),
        cost_estimate=pl.CostEstimate(
            flops=2 * lanes * rows_dev * cols_dev,
            bytes_accessed=2 * rows_dev * cols_dev,
            transcendentals=0,
        ),
        name="order_sums",
    )(orders, covariance)


def columns_kernel(own, near, outer, far, table, result, partial, rhs):
    for s, ref in enumerate((own, near, outer, far)):
        n = ref.shape[0]
        rhs[s * n : (s + 1) * n, :] = ref[...]
    both = dot3(split(table[...]), split(rhs[...]), ((1,), (0,)))
    n = result.shape[0]
    result[...] = both[:n]
    partial[...] = both[n:]


def columns(own, near, outer, far, table):
    n, lanes = table.shape[0] // 2, own.shape[1]
    out = jax.ShapeDtypeStruct((n, lanes), F32)
    return pl.pallas_call(
        columns_kernel,
        out_shape=[out, out],
        in_specs=[pl.BlockSpec(memory_space=pltpu.VMEM)] * 5,
        out_specs=[pl.BlockSpec(memory_space=pltpu.VMEM)] * 2,
        scratch_shapes=[pltpu.VMEM((4 * own.shape[0], lanes), F32)],
        compiler_params=pltpu.CompilerParams(vmem_limit_bytes=32 * 1024 * 1024),
        cost_estimate=pl.CostEstimate(
            flops=6 * table.size * lanes, bytes_accessed=16 * own.size, transcendentals=0
        ),
        name="columns",
    )(own, near, outer, far, table)


def rows_kernel(mine, other, table, *refs):
    outs, turned = refs[:CHIPS], refs[CHIPS]
    n, lanes = mine.shape
    part = lanes // CHIPS
    for c, ref in enumerate((mine, other)):
        for g in range(NLAT // 4):
            xs = [ref[:, d * part + g * LL : d * part + (g + 1) * LL] for d in range(CHIPS)]
            for u, y in enumerate(turn4(xs)):
                turned[c, pl.ds(4 * g + u, n, stride=NLAT), :] = y
    values = jnp.concatenate([turned[0], turned[1]], axis=1)
    grid = dot3(split(table[...]), split(values), ((1,), (1,)))
    m = table.shape[0] // CHIPS
    for d in range(CHIPS):
        outs[d][...] = grid[d * m : (d + 1) * m]


def rows(mine, other, table):
    n, lanes = mine.shape
    m = table.shape[0] // CHIPS
    out = jax.ShapeDtypeStruct((m, n * NLAT), F32)
    return pl.pallas_call(
        rows_kernel,
        out_shape=[out] * CHIPS,
        in_specs=[pl.BlockSpec(memory_space=pltpu.VMEM)] * 3,
        out_specs=[pl.BlockSpec(memory_space=pltpu.VMEM)] * CHIPS,
        scratch_shapes=[pltpu.VMEM((2, n * NLAT, LL), F32)],
        compiler_params=pltpu.CompilerParams(vmem_limit_bytes=32 * 1024 * 1024),
        cost_estimate=pl.CostEstimate(
            flops=6 * table.size * n * NLAT, bytes_accessed=16 * mine.size, transcendentals=0
        ),
        name="rows",
    )(mine, other, table)


def place_kernel(*refs):
    parts, out, held = refs[:-2], refs[-2], refs[-1]
    tiles = held.shape[0]
    chip = lax.axis_index("row") // 2
    for t in range(CHUNKS):
        for d in range(CHIPS):
            ref = parts[t * CHIPS + d]
            row = 4 * t + lax.bitwise_xor(chip, d)
            for h in range(tiles):
                held[h, pl.ds(row, ref.shape[0], stride=NLAT), :] = ref[:, h * LL : (h + 1) * LL]
    for h in range(tiles):
        out[:, h * LL : (h + 1) * LL] = held[h]


def place(parts):
    m, lanes = parts[0].shape
    return pl.pallas_call(
        place_kernel,
        out_shape=jax.ShapeDtypeStruct((m * NLAT, lanes), F32),
        in_specs=[pl.BlockSpec(memory_space=pltpu.VMEM)] * len(parts),
        out_specs=pl.BlockSpec(memory_space=pltpu.VMEM),
        scratch_shapes=[pltpu.VMEM((lanes // LL, m * NLAT, LL), F32)],
        compiler_params=pltpu.CompilerParams(vmem_limit_bytes=32 * 1024 * 1024),
        name="place",
    )(*parts)


def wave(lons, keys):
    turns = (lons[:, None] * (keys // 2)[None, :] + (NLON // 4) * (1 - keys % 2)[None, :]) % NLON
    return jnp.sin(turns.astype(F32) * (2.0 * math.pi / NLON))


def tables(orders):
    row_place, col_place = lax.axis_index("row"), lax.axis_index("col")
    row_count, col_count = lax.axis_size("row"), lax.axis_size("col")
    second = jnp.where(orders == 0, LL // 2, LL - orders)
    keys = jnp.stack([2 * orders, 2 * orders + 1, 2 * second, 2 * second + 1], 1).reshape(-1)
    by_col = keys.reshape(col_count, -1)
    pick = lambda table, index: lax.dynamic_index_in_dim(table, index, 0, keepdims=False)
    col_keys = jnp.concatenate([pick(by_col, col_place ^ s) for s in (0, 3, 1, 2)])
    lons = jnp.arange(NLON // col_count, dtype=jnp.int32)
    col_lons = jnp.concatenate([lons + (col_place ^ s) * lons.size for s in (0, 1)])
    col_table = wave(col_lons, col_keys)
    n = by_col.shape[1]
    hidden = (jnp.arange(2 * lons.size) >= lons.size)[:, None] & (
        (jnp.arange(4 * n) // n) == 2
    )[None, :]
    col_table = jnp.where(hidden, 0.0, col_table)
    by_row = keys.reshape(row_count, -1)
    row_keys = jnp.concatenate(
        [pick(by_row, row_place ^ (2 * d + c)) for c in range(2) for d in range(CHIPS)]
    )
    lons = jnp.arange(NLON // row_count, dtype=jnp.int32)
    row_lons = jnp.concatenate(
        [lons + (row_place ^ (2 * d)) * lons.size for d in range(CHIPS)]
    )
    return col_table, wave(row_lons, row_keys)


def chunked(covariance, coef_index):
    orders = coef_index[1].reshape(-1, PAIR)[:, 0]
    sums = order_sums(covariance, orders)
    orders, *sums = lax.optimization_barrier((orders, *sums))
    col_table, row_table = tables(orders)
    flip = lambda x, bits: lax.ppermute(
        x, "row", [(r, r ^ bits) for r in range(lax.axis_size("row"))]
    )
    along = lambda x, *pairs: lax.ppermute(x, "col", pairs)
    parts = []
    for t in range(CHUNKS):
        mine = sums[t * CHIPS : (t + 1) * CHIPS]
        own = jnp.concatenate(
            [mine[0]] + [flip(mine[d], 2 * d) for d in range(1, CHIPS)], axis=1
        )
        near = along(own, (1, 2), (2, 1))
        outer = along(own, (0, 1), (3, 2))
        far = along(outer, (1, 2), (2, 1))
        result, partial = columns(own, near, outer, far, col_table)
        result = result + along(partial, (1, 0), (2, 3))
        grid = rows(result, flip(result, 1), row_table)
        parts += [grid[0]] + [flip(grid[d], 2 * d) for d in range(1, CHIPS)]
    return place(parts)


def legendre_rows(lat_count, lon_count, degree_count):
    grid_rows = lon_count // 2
    first_row = grid_rows // 2 - lat_count // 2
    colatitude = (first_row + jnp.arange(lat_count, dtype=jnp.float32) + 0.5) * (
        math.pi / grid_rows
    )
    cosine = jnp.cos(colatitude)[:, None]
    sine_vals = jnp.sin(colatitude)[:, None]
    orders = jnp.arange(degree_count, dtype=jnp.float32)[None, :]
    growth = jnp.sqrt((2.0 * orders + 1.0) / jnp.maximum(2.0 * orders, 1.0))
    growth = jnp.where(
        orders == 1.0, jnp.sqrt(jnp.float32(3.0)), jnp.where(orders == 0.0, 1.0, growth)
    )
    sectoral = jnp.exp(jnp.cumsum(jnp.log(growth), axis=1) + orders * jnp.log(sine_vals))

    def advance(state_pair, degree):
        before, earlier = state_pair
        deg_sum = degree + orders
        deg_diff = degree - orders
        alpha_lm = jnp.sqrt(
            jnp.maximum((2.0 * degree - 1.0) * (2.0 * degree + 1.0), 0.0)
            / jnp.maximum(deg_diff * deg_sum, 1.0)
        )
        beta_lm = jnp.sqrt(
            jnp.maximum((2.0 * degree + 1.0) * (deg_sum - 1.0) * (deg_diff - 1.0), 0.0)
            / jnp.maximum(deg_diff * deg_sum * (2.0 * degree - 3.0), 1.0)
        )
        general = alpha_lm * cosine * before - beta_lm * earlier
        current = jnp.where(orders < degree, general, jnp.where(orders == degree, sectoral, 0.0))
        return ((current, before), current)

    start_pair = (
        jnp.zeros((lat_count, degree_count), jnp.float32),
        jnp.zeros((lat_count, degree_count), jnp.float32),
    )
    _, stacked = lax.scan(
        advance, start_pair, jnp.arange(degree_count, dtype=jnp.float32), unroll=16
    )
    return jnp.transpose(stacked, (1, 0, 2)).reshape(lat_count, degree_count * degree_count)


def fourier(modes, parity, longitudes):
    phases = longitudes[:, None] * modes[None, :] % NLON
    angles = phases.astype(jnp.float32) * (2.0 * math.pi / NLON)
    return jnp.where(parity[None, :] == 0, jnp.cos(angles), jnp.sin(angles))


def block_slots(orders_flat, blocks, length, slot_count):
    grouped = orders_flat.reshape(blocks, length)
    change = jnp.concatenate(
        [jnp.ones((blocks, 1), jnp.int32), (grouped[:, 1:] != grouped[:, :-1]).astype(jnp.int32)],
        axis=1,
    )
    slot_ids = jnp.cumsum(change, axis=1) - 1
    first_marks = (
        slot_ids[:, :, None] == jnp.arange(slot_count, dtype=jnp.int32)[None, None, :]
    ) & (change[:, :, None] == 1)
    firsts = jnp.sum(jnp.where(first_marks, grouped[:, :, None], 0), axis=1)
    return (slot_ids, firsts)


def spectral_weights(plm_table, degree, orders, parity, slot_ids, slot_count):
    values = plm_table[:, degree * LL + orders]
    key_ids = 2 * slot_ids + parity
    matches = key_ids[None, None, :] == jnp.arange(2 * slot_count, dtype=jnp.int32)[None, :, None]
    return jnp.where(matches, values[:, None, :], 0.0)


def on_device(covariance, coef_index):
    rows_dev, cols_dev = covariance.shape
    row_count = lax.axis_size("row")
    col_count = lax.axis_size("col")
    row_place = lax.axis_index("row")
    col_place = lax.axis_index("col")
    row_orders = max(LL // row_count, 2)
    col_orders = max(LL // col_count, 2)
    plm_table = legendre_rows(NLAT, NLON, LL)
    row_slots, row_firsts = block_slots(coef_index[1], row_count, rows_dev, row_orders)
    col_slots, col_firsts = block_slots(coef_index[1], col_count, cols_dev, col_orders)
    mine_rows = lax.dynamic_slice_in_dim(coef_index, row_place * rows_dev, rows_dev, 1)
    mine_cols = lax.dynamic_slice_in_dim(coef_index, col_place * cols_dev, cols_dev, 1)
    own_row_slots = lax.dynamic_index_in_dim(row_slots, row_place, 0, keepdims=False)
    own_col_slots = lax.dynamic_index_in_dim(col_slots, col_place, 0, keepdims=False)
    row_weights = spectral_weights(
        plm_table, mine_rows[0], mine_rows[1], mine_rows[2], own_row_slots, row_orders
    )
    row_weights = row_weights.astype(jnp.bfloat16).reshape(NLAT * 2 * row_orders, rows_dev)
    col_weights = spectral_weights(
        plm_table, mine_cols[0], mine_cols[1], mine_cols[2], own_col_slots, col_orders
    )
    first_pass = jnp.dot(row_weights, covariance, preferred_element_type=jnp.float32)
    second = jnp.einsum("ak,jbk->ajb", first_pass, col_weights, precision=lax.Precision.HIGHEST)
    width_cols = NLAT * 2 * col_orders
    second = second.reshape(NLAT, 2 * row_orders, width_cols)
    all_lons = jnp.arange(NLON, dtype=jnp.int32)
    row_modes = jnp.repeat(row_firsts.reshape(-1), 2)
    row_parity = jnp.arange(row_modes.shape[0], dtype=jnp.int32) % 2
    row_table = fourier(row_modes, row_parity, all_lons)
    grid_vals = jnp.einsum(
        "jq,iqc->jic",
        row_table,
        lax.all_to_all(second, "row", split_axis=2, concat_axis=1, tiled=True),
        precision=lax.Precision.HIGHEST,
    )
    row_done = lax.all_to_all(grid_vals, "row", split_axis=0, concat_axis=2, tiled=True)
    pts_row = row_done.shape[0] * NLAT
    spectral = row_done.reshape(pts_row, NLAT, 2 * col_orders)
    own_modes = jnp.repeat(lax.dynamic_index_in_dim(col_firsts, col_place, 0, keepdims=False), 2)
    own_parity = jnp.arange(2 * col_orders, dtype=jnp.int32) % 2
    pts_col = NLAT * NLON // col_count
    longitudes = jnp.arange(pts_col * lax.axis_size("col") // NLAT, dtype=jnp.int32)
    table_part = fourier(own_modes, own_parity, longitudes)
    grid_vals = jnp.einsum("jk,pik->jip", table_part, spectral, precision=lax.Precision.HIGHEST)
    summed = lax.psum_scatter(
        grid_vals.reshape(pts_col * lax.axis_size("col"), pts_row),
        "col",
        scatter_dimension=0,
        tiled=True,
    )
    result = summed.T
    return result


def solution(mesh):
    in_specs = (P("row", "col"), P())
    out_specs = P("row", "col")
    fits = mesh.shape["row"] == 2 * CHIPS and mesh.shape["col"] == 4
    return jax.shard_map(
        chunked if fits else on_device, mesh=mesh, in_specs=in_specs, out_specs=out_specs, check_vma=False
    )
```

```python
import functools
import math

import jax
import jax.numpy as jnp
from jax import lax
from jax.experimental import pallas as pl
from jax.experimental.pallas import tpu as pltpu
from jax.sharding import PartitionSpec as P

LL = 128
NLON = 384
NLAT = 12

F32 = jnp.float32
BF16 = jnp.bfloat16
ROWS16 = 16
CHIPS = 4
CHUNKS = NLAT // CHIPS
PAIR = 2 * LL
KEYS = 4
STEP = 2 * PAIR
GROUP = 2


def split(x):
    high = x.astype(BF16)
    return high, (x - high.astype(F32)).astype(BF16)


def dot3(a, b, dims):
    dg = functools.partial(
        lax.dot_general, dimension_numbers=(dims, ((), ())), preferred_element_type=F32
    )
    return dg(a[0], b[0]) + (dg(a[0], b[1]) + dg(a[1], b[0]))


def turn4(xs):
    lane = lax.broadcasted_iota(jnp.int32, xs[0].shape, 1)
    left = lane < 64
    even = (lane // 32) % 2 == 0
    out = [None] * 4
    halves = []
    for u in range(2):
        a, b = xs[u], xs[u + 2]
        halves.append(
            (jnp.where(left, a, pltpu.roll(b, 64, 1)), jnp.where(left, pltpu.roll(a, 64, 1), b))
        )
    for h in range(2):
        a, b = halves[0][h], halves[1][h]
        out[2 * h] = jnp.where(even, a, pltpu.roll(b, 32, 1))
        out[2 * h + 1] = jnp.where(even, pltpu.roll(a, 96, 1), b)
    return out


def legendre_table(by_degree, by_order):
    shape = (ROWS16, LL)
    lat = lax.broadcasted_iota(jnp.int32, shape, 0).astype(F32)
    colatitude = (NLON // 4 - NLAT // 2 + lat + 0.5) * (math.pi / (NLON // 2))
    cosine, sine = jnp.cos(colatitude), jnp.sin(colatitude)
    lane = lax.broadcasted_iota(jnp.int32, shape, 1)
    orders = lane.astype(F32)
    growth = jnp.sqrt((2.0 * orders + 1.0) / jnp.maximum(2.0 * orders, 1.0))
    growth = jnp.where(lane == 1, math.sqrt(3.0), jnp.where(lane == 0, 1.0, growth))
    total = jnp.log(growth)
    shift = 1
    while shift < LL:
        total = total + jnp.where(lane >= shift, pltpu.roll(total, shift, 1), 0.0)
        shift *= 2
    sectoral = jnp.exp(total + orders * jnp.log(sine))
    m8 = lax.broadcasted_iota(jnp.int32, (8, LL), 1).astype(F32)
    r8 = lax.broadcasted_iota(jnp.int32, (8, LL), 0)

    def block(b, carry):
        before, earlier = carry
        degree = (r8 + b * 8).astype(F32)
        plus, minus = degree + m8, degree - m8
        alpha = jnp.sqrt(
            jnp.maximum((2.0 * degree - 1.0) * (2.0 * degree + 1.0), 0.0)
            / jnp.maximum(minus * plus, 1.0)
        )
        beta = jnp.sqrt(
            jnp.maximum((2.0 * degree + 1.0) * (plus - 1.0) * (minus - 1.0), 0.0)
            / jnp.maximum(minus * plus * (2.0 * degree - 3.0), 1.0)
        )
        for r in range(8):
            l = b * 8 + r
            general = alpha[r : r + 1] * cosine * before - beta[r : r + 1] * earlier
            current = jnp.where(lane < l, general, jnp.where(lane == l, sectoral, 0.0))
            by_degree[pl.ds(pl.multiple_of(l * ROWS16, ROWS16), ROWS16), :] = current
            before, earlier = current, before
        return before, earlier

    zeros = jnp.zeros(shape, F32)
    lax.fori_loop(0, LL // 8, block, (zeros, zeros))
    for i in range(NLAT):
        by_order[pl.ds(i, LL, stride=ROWS16), :] = by_degree[pl.ds(i, LL, stride=ROWS16), :].T


def pair_weights(by_order, first, arrange):
    second = jnp.where(first == 0, LL // 2, LL - first)
    at = lambda m: arrange(by_order[pl.ds(pl.multiple_of(m * ROWS16, ROWS16), ROWS16), :])
    va, vb = at(first), at(second)
    na, nb = LL - first, LL - second
    lane = lax.broadcasted_iota(jnp.int32, va.shape, 1)
    wrap = lambda s: lax.bitwise_and(s, LL - 1)
    sines = pltpu.roll(va, wrap(2 * na), 1)
    real = first > 0
    begin = wrap(2 * na)
    return (
        (pltpu.roll(va, wrap(na), 1), None),
        (
            jnp.where((lane >= na) & real, sines, 0.0),
            jnp.where((lane < na) & real, sines, 0.0),
        ),
        (None, pltpu.roll(vb, wrap(nb + begin), 1)),
        (None, pltpu.roll(vb, wrap(2 * nb + begin), 1)),
    )


def order_sums_kernel(row_pairs, col_pairs, steps, index, cov, *refs):
    first_out, later_outs = refs[0], refs[1 : 1 + CHIPS]
    (
        held, by_degree, by_order, row_w, row_wb, col_w, col_wb, even, odd, second, orders, sems, order_sem
    ) = refs[1 + CHIPS :]
    row_place, col_place = lax.axis_index("row"), lax.axis_index("col")
    chip = row_place // 2
    pairs = [row_place * row_pairs + p for p in range(row_pairs)]
    pairs += [col_place * col_pairs + p for p in range(col_pairs)]
    heads = [
        pltpu.make_async_copy(
            index.at[1:2, pl.ds(pl.multiple_of(p * PAIR, PAIR), LL)],
            orders.at[n : n + 1, :],
            order_sem.at[n],
        )
        for n, p in enumerate(pairs)
    ]
    for head in heads:
        head.start()
    copy = lambda s: pltpu.make_async_copy(
        cov.at[:, pl.ds(pl.multiple_of(s * STEP, STEP), STEP)], held.at[s], sems.at[s]
    )
    for s in range(steps):
        copy(s).start()
    legendre_table(by_degree, by_order)
    for head in heads:
        head.wait()
    row_w[...] = jnp.zeros_like(row_w)
    col_w[...] = jnp.zeros_like(col_w)

    def own_first(v):
        place = lax.broadcasted_iota(jnp.int32, v.shape, 0)
        for bit in (1, 2):
            up = pltpu.roll(v, ROWS16 - bit, 0)
            down = pltpu.roll(v, bit, 0)
            swapped = jnp.where(lax.bitwise_and(place, bit) == 0, up, down)
            v = jnp.where(lax.bitwise_and(chip, bit) == 0, v, swapped)
        return v

    for p in range(row_pairs):
        for k, sides in enumerate(pair_weights(by_order, orders[p, 0], own_first)):
            for h, v in enumerate(sides):
                if v is not None:
                    row_w[
                        p % GROUP * 2 + h, pl.ds(p * KEYS * NLAT + k, NLAT, stride=KEYS), :
                    ] = v[:NLAT]
    for h in range(2 * GROUP):
        row_wb[:, h * LL : (h + 1) * LL] = row_w[h].astype(BF16)
    for p in range(col_pairs):
        s, e = p // 2, p % 2
        for k, sides in enumerate(
            pair_weights(by_order, orders[row_pairs + p, 0], lambda v: v)
        ):
            for h, v in enumerate(sides):
                if v is not None:
                    col_w[
                        2 * e + h, pl.ds(s * LL + e * KEYS + k, NLAT, stride=2 * KEYS), :
                    ] = v[:NLAT]
    for s in range(steps):
        for h in range(4):
            high, low = split(col_w[h, s * LL : (s + 1) * LL, :].T)
            col_wb[s, h * LL : (h + 1) * LL, :LL] = high
            col_wb[s, h * LL : (h + 1) * LL, LL:] = low

    def column_side(s, half):
        both = lax.dot_general(
            held[s], col_wb[s], (((1,), (0,)), ((), ())), preferred_element_type=F32
        )
        high, low = split(both[:, :LL] + both[:, LL:])
        half[:, :LL] = high
        half[:, LL:] = low

    def row_side(s, half):
        rows = GROUP * KEYS * NLAT
        for q in range(row_pairs // GROUP):
            both = jnp.dot(
                row_wb[q * rows : (q + 1) * rows, :],
                half[q * GROUP * PAIR : (q + 1) * GROUP * PAIR, :],
                preferred_element_type=F32,
            )
            both = both[:, :LL] + both[:, LL:]
            for g in range(GROUP):
                for i in range(NLAT):
                    row = (i * row_pairs + q * GROUP + g) * KEYS
                    from_row = (g * NLAT + i) * KEYS
                    second[row : row + KEYS, :] = both[from_row : from_row + KEYS]
        part = row_pairs * KEYS * NLAT
        for t in range(CHUNKS):
            turned = second[t * LL : (t + 1) * LL, :].T
            for g in range(NLAT // 4):
                xs = [turned[8 * (4 * g + u) : 8 * (4 * g + u + 1)] for u in range(4)]
                for d, x in enumerate(turn4(xs)):
                    lanes = slice(g * LL, (g + 1) * LL)
                    if t == 0:
                        lanes = slice(d * part + g * LL, d * part + (g + 1) * LL)
                        first_out[pl.ds(pl.multiple_of(s * 8, 8), 8), lanes] = x
                    else:
                        row = (t - 1) * steps * 8 + s * 8
                        later_outs[d][pl.ds(pl.multiple_of(row, 8), 8), lanes] = x

    def both_sides(s, now, later):
        copy(s + 1).wait()
        column_side(s + 1, later)
        row_side(s, now)

    def step(j, carry):
        both_sides(2 * j, even, odd)
        both_sides(2 * j + 1, odd, even)
        return carry

    copy(0).wait()
    column_side(0, even)
    lax.fori_loop(0, steps // 2 - 1, step, 0)
    both_sides(steps - 2, even, odd)
    row_side(steps - 1, odd)


def order_sums(covariance, coef_index):
    rows_dev, cols_dev = covariance.shape
    row_pairs, col_pairs, steps = rows_dev // PAIR, cols_dev // PAIR, cols_dev // STEP
    lanes, keys = NLAT * row_pairs * KEYS, col_pairs * KEYS
    later = jax.ShapeDtypeStruct(((CHUNKS - 1) * keys, lanes), F32)
    return pl.pallas_call(
        functools.partial(order_sums_kernel, row_pairs, col_pairs, steps),
        out_shape=[jax.ShapeDtypeStruct((keys, CHIPS * lanes), F32)] + [later] * CHIPS,
        in_specs=[pl.BlockSpec(memory_space=pl.ANY)] * 2,
        out_specs=[pl.BlockSpec(memory_space=pltpu.VMEM)] * (1 + CHIPS),
        scratch_shapes=[
            pltpu.VMEM((steps, rows_dev, STEP), BF16),
            pltpu.VMEM((LL * ROWS16, LL), F32),
            pltpu.VMEM((LL * ROWS16, LL), F32),
            pltpu.VMEM((2 * GROUP, lanes, LL), F32),
            pltpu.VMEM((lanes, GROUP * PAIR), BF16),
            pltpu.VMEM((STEP // LL, steps * LL, LL), F32),
            pltpu.VMEM((steps, STEP, 2 * LL), BF16),
            pltpu.VMEM((rows_dev, 2 * LL), BF16),
            pltpu.VMEM((rows_dev, 2 * LL), BF16),
            pltpu.VMEM((lanes, LL), F32),
            pltpu.SMEM((row_pairs + col_pairs, LL), jnp.int32),
            pltpu.SemaphoreType.DMA((steps,)),
            pltpu.SemaphoreType.DMA((row_pairs + col_pairs,)),
        ],
        compiler_params=pltpu.CompilerParams(vmem_limit_bytes=56 * 1024 * 1024),
        cost_estimate=pl.CostEstimate(
            flops=2 * lanes * rows_dev * cols_dev,
            bytes_accessed=2 * rows_dev * cols_dev,
            transcendentals=0,
        ),
        name="order_sums",
    )(coef_index, covariance)


def columns_kernel(own, near, outer, far, table, result, partial, rhs):
    for s, ref in enumerate((own, near, outer, far)):
        n = ref.shape[0]
        rhs[s * n : (s + 1) * n, :] = ref[...]
    both = dot3(split(table[...]), split(rhs[...]), ((1,), (0,)))
    n = result.shape[0]
    result[...] = both[:n]
    partial[...] = both[n:]


def columns(own, near, outer, far, table):
    n, lanes = table.shape[0] // 2, own.shape[1]
    out = jax.ShapeDtypeStruct((n, lanes), F32)
    return pl.pallas_call(
        columns_kernel,
        out_shape=[out, out],
        in_specs=[pl.BlockSpec(memory_space=pltpu.VMEM)] * 5,
        out_specs=[pl.BlockSpec(memory_space=pltpu.VMEM)] * 2,
        scratch_shapes=[pltpu.VMEM((4 * own.shape[0], lanes), F32)],
        compiler_params=pltpu.CompilerParams(vmem_limit_bytes=32 * 1024 * 1024),
        cost_estimate=pl.CostEstimate(
            flops=6 * table.size * lanes, bytes_accessed=16 * own.size, transcendentals=0
        ),
        name="columns",
    )(own, near, outer, far, table)


def rows_kernel(mine, other, table, *refs):
    outs, turned = refs[:CHIPS], refs[CHIPS]
    n, lanes = mine.shape
    part = lanes // CHIPS
    for c, ref in enumerate((mine, other)):
        for g in range(NLAT // 4):
            xs = [ref[:, d * part + g * LL : d * part + (g + 1) * LL] for d in range(CHIPS)]
            for u, y in enumerate(turn4(xs)):
                turned[c, pl.ds(4 * g + u, n, stride=NLAT), :] = y
    values = jnp.concatenate([turned[0], turned[1]], axis=1)
    grid = dot3(split(table[...]), split(values), ((1,), (1,)))
    m = table.shape[0] // CHIPS
    for d in range(CHIPS):
        outs[d][...] = grid[d * m : (d + 1) * m]


def rows(mine, other, table):
    n, lanes = mine.shape
    m = table.shape[0] // CHIPS
    out = jax.ShapeDtypeStruct((m, n * NLAT), F32)
    return pl.pallas_call(
        rows_kernel,
        out_shape=[out] * CHIPS,
        in_specs=[pl.BlockSpec(memory_space=pltpu.VMEM)] * 3,
        out_specs=[pl.BlockSpec(memory_space=pltpu.VMEM)] * CHIPS,
        scratch_shapes=[pltpu.VMEM((2, n * NLAT, LL), F32)],
        compiler_params=pltpu.CompilerParams(vmem_limit_bytes=32 * 1024 * 1024),
        cost_estimate=pl.CostEstimate(
            flops=6 * table.size * n * NLAT, bytes_accessed=16 * mine.size, transcendentals=0
        ),
        name="rows",
    )(mine, other, table)


def place_kernel(*refs):
    parts, out, held = refs[:-2], refs[-2], refs[-1]
    tiles = held.shape[0]
    chip = lax.axis_index("row") // 2
    for t in range(CHUNKS):
        for d in range(CHIPS):
            ref = parts[t * CHIPS + d]
            row = 4 * t + lax.bitwise_xor(chip, d)
            for h in range(tiles):
                held[h, pl.ds(row, ref.shape[0], stride=NLAT), :] = ref[:, h * LL : (h + 1) * LL]
    for h in range(tiles):
        out[:, h * LL : (h + 1) * LL] = held[h]


def place(parts):
    m, lanes = parts[0].shape
    return pl.pallas_call(
        place_kernel,
        out_shape=jax.ShapeDtypeStruct((m * NLAT, lanes), F32),
        in_specs=[pl.BlockSpec(memory_space=pltpu.VMEM)] * len(parts),
        out_specs=pl.BlockSpec(memory_space=pltpu.VMEM),
        scratch_shapes=[pltpu.VMEM((lanes // LL, m * NLAT, LL), F32)],
        compiler_params=pltpu.CompilerParams(vmem_limit_bytes=32 * 1024 * 1024),
        name="place",
    )(*parts)


def wave(lons, keys):
    turns = (lons[:, None] * (keys // 2)[None, :] + (NLON // 4) * (1 - keys % 2)[None, :]) % NLON
    return jnp.sin(turns.astype(F32) * (2.0 * math.pi / NLON))


def tables(orders):
    row_place, col_place = lax.axis_index("row"), lax.axis_index("col")
    row_count, col_count = lax.axis_size("row"), lax.axis_size("col")
    second = jnp.where(orders == 0, LL // 2, LL - orders)
    keys = jnp.stack([2 * orders, 2 * orders + 1, 2 * second, 2 * second + 1], 1).reshape(-1)
    by_col = keys.reshape(col_count, -1)
    pick = lambda table, index: lax.dynamic_index_in_dim(table, index, 0, keepdims=False)
    col_keys = jnp.concatenate([pick(by_col, col_place ^ s) for s in (0, 3, 1, 2)])
    lons = jnp.arange(NLON // col_count, dtype=jnp.int32)
    col_lons = jnp.concatenate([lons + (col_place ^ s) * lons.size for s in (0, 1)])
    col_table = wave(col_lons, col_keys)
    n = by_col.shape[1]
    hidden = (jnp.arange(2 * lons.size) >= lons.size)[:, None] & (
        (jnp.arange(4 * n) // n) == 2
    )[None, :]
    col_table = jnp.where(hidden, 0.0, col_table)
    by_row = keys.reshape(row_count, -1)
    row_keys = jnp.concatenate(
        [pick(by_row, row_place ^ (2 * d + c)) for c in range(2) for d in range(CHIPS)]
    )
    lons = jnp.arange(NLON // row_count, dtype=jnp.int32)
    row_lons = jnp.concatenate(
        [lons + (row_place ^ (2 * d)) * lons.size for d in range(CHIPS)]
    )
    return col_table, wave(row_lons, row_keys)


def after(x, *done):
    return lax.optimization_barrier((x, *done))[0]


def chunked(covariance, coef_index):
    flip = lambda x, bits: lax.ppermute(
        x, "row", [(r, r ^ bits) for r in range(lax.axis_size("row"))]
    )
    along = lambda x, *pairs: lax.ppermute(x, "col", pairs)

    def spread(xs):
        return [xs[0]] + [flip(xs[d], 2 * d) for d in range(1, CHIPS)]

    def inward(own):
        outer = along(own, (0, 1), (3, 2))
        return along(own, (1, 2), (2, 1)), outer

    def across(outer):
        return along(outer, (1, 2), (2, 1))

    def outward(result, partial):
        return result + along(partial, (1, 0), (2, 3))

    def finish(result):
        return spread(rows(result, flip(result, 1), row_table))

    own0, *later = order_sums(covariance, coef_index)
    orders = after(coef_index, own0)[1].reshape(-1, PAIR)[:, 0]
    col_table, row_table = tables(orders)
    near0, outer0 = inward(own0)
    later = spread(later)
    far0 = across(outer0)
    keys = own0.shape[0]
    own1, own2 = (
        jnp.concatenate([x[t * keys : (t + 1) * keys] for x in later], axis=1) for t in range(2)
    )
    near1, outer1 = inward(after(own1, near0, outer0))
    result0, partial0 = columns(own0, near0, outer0, far0, col_table)
    far1 = across(after(outer1, far0))
    near2, outer2 = inward(after(own2, near1, outer1, partial0))
    result0 = outward(result0, partial0)
    result1, partial1 = columns(own1, near1, outer1, far1, col_table)
    far2 = across(after(outer2, result0, partial1))
    lanes = result0.shape[1] // CHIPS
    result0 = jnp.concatenate(
        spread([result0[:, d * lanes : (d + 1) * lanes] for d in range(CHIPS)]), axis=1
    )
    result2, partial2 = columns(own2, near2, outer2, far2, after(col_table, result0))
    result1 = outward(result1, partial1)
    grid0 = finish(result0)
    result2 = outward(result2, after(partial2, result1))
    grid1 = finish(result1)
    grid2 = finish(after(result2, *grid0))
    return place(grid0 + grid1 + grid2)


def legendre_rows(lat_count, lon_count, degree_count):
    grid_rows = lon_count // 2
    first_row = grid_rows // 2 - lat_count // 2
    colatitude = (first_row + jnp.arange(lat_count, dtype=jnp.float32) + 0.5) * (
        math.pi / grid_rows
    )
    cosine = jnp.cos(colatitude)[:, None]
    sine_vals = jnp.sin(colatitude)[:, None]
    orders = jnp.arange(degree_count, dtype=jnp.float32)[None, :]
    growth = jnp.sqrt((2.0 * orders + 1.0) / jnp.maximum(2.0 * orders, 1.0))
    growth = jnp.where(
        orders == 1.0, jnp.sqrt(jnp.float32(3.0)), jnp.where(orders == 0.0, 1.0, growth)
    )
    sectoral = jnp.exp(jnp.cumsum(jnp.log(growth), axis=1) + orders * jnp.log(sine_vals))

    def advance(state_pair, degree):
        before, earlier = state_pair
        deg_sum = degree + orders
        deg_diff = degree - orders
        alpha_lm = jnp.sqrt(
            jnp.maximum((2.0 * degree - 1.0) * (2.0 * degree + 1.0), 0.0)
            / jnp.maximum(deg_diff * deg_sum, 1.0)
        )
        beta_lm = jnp.sqrt(
            jnp.maximum((2.0 * degree + 1.0) * (deg_sum - 1.0) * (deg_diff - 1.0), 0.0)
            / jnp.maximum(deg_diff * deg_sum * (2.0 * degree - 3.0), 1.0)
        )
        general = alpha_lm * cosine * before - beta_lm * earlier
        current = jnp.where(orders < degree, general, jnp.where(orders == degree, sectoral, 0.0))
        return ((current, before), current)

    start_pair = (
        jnp.zeros((lat_count, degree_count), jnp.float32),
        jnp.zeros((lat_count, degree_count), jnp.float32),
    )
    _, stacked = lax.scan(
        advance, start_pair, jnp.arange(degree_count, dtype=jnp.float32), unroll=16
    )
    return jnp.transpose(stacked, (1, 0, 2)).reshape(lat_count, degree_count * degree_count)


def fourier(modes, parity, longitudes):
    phases = longitudes[:, None] * modes[None, :] % NLON
    angles = phases.astype(jnp.float32) * (2.0 * math.pi / NLON)
    return jnp.where(parity[None, :] == 0, jnp.cos(angles), jnp.sin(angles))


def block_slots(orders_flat, blocks, length, slot_count):
    grouped = orders_flat.reshape(blocks, length)
    change = jnp.concatenate(
        [jnp.ones((blocks, 1), jnp.int32), (grouped[:, 1:] != grouped[:, :-1]).astype(jnp.int32)],
        axis=1,
    )
    slot_ids = jnp.cumsum(change, axis=1) - 1
    first_marks = (
        slot_ids[:, :, None] == jnp.arange(slot_count, dtype=jnp.int32)[None, None, :]
    ) & (change[:, :, None] == 1)
    firsts = jnp.sum(jnp.where(first_marks, grouped[:, :, None], 0), axis=1)
    return (slot_ids, firsts)


def spectral_weights(plm_table, degree, orders, parity, slot_ids, slot_count):
    values = plm_table[:, degree * LL + orders]
    key_ids = 2 * slot_ids + parity
    matches = key_ids[None, None, :] == jnp.arange(2 * slot_count, dtype=jnp.int32)[None, :, None]
    return jnp.where(matches, values[:, None, :], 0.0)


def on_device(covariance, coef_index):
    rows_dev, cols_dev = covariance.shape
    row_count = lax.axis_size("row")
    col_count = lax.axis_size("col")
    row_place = lax.axis_index("row")
    col_place = lax.axis_index("col")
    row_orders = max(LL // row_count, 2)
    col_orders = max(LL // col_count, 2)
    plm_table = legendre_rows(NLAT, NLON, LL)
    row_slots, row_firsts = block_slots(coef_index[1], row_count, rows_dev, row_orders)
    col_slots, col_firsts = block_slots(coef_index[1], col_count, cols_dev, col_orders)
    mine_rows = lax.dynamic_slice_in_dim(coef_index, row_place * rows_dev, rows_dev, 1)
    mine_cols = lax.dynamic_slice_in_dim(coef_index, col_place * cols_dev, cols_dev, 1)
    own_row_slots = lax.dynamic_index_in_dim(row_slots, row_place, 0, keepdims=False)
    own_col_slots = lax.dynamic_index_in_dim(col_slots, col_place, 0, keepdims=False)
    row_weights = spectral_weights(
        plm_table, mine_rows[0], mine_rows[1], mine_rows[2], own_row_slots, row_orders
    )
    row_weights = row_weights.astype(jnp.bfloat16).reshape(NLAT * 2 * row_orders, rows_dev)
    col_weights = spectral_weights(
        plm_table, mine_cols[0], mine_cols[1], mine_cols[2], own_col_slots, col_orders
    )
    first_pass = jnp.dot(row_weights, covariance, preferred_element_type=jnp.float32)
    second = jnp.einsum("ak,jbk->ajb", first_pass, col_weights, precision=lax.Precision.HIGHEST)
    width_cols = NLAT * 2 * col_orders
    second = second.reshape(NLAT, 2 * row_orders, width_cols)
    all_lons = jnp.arange(NLON, dtype=jnp.int32)
    row_modes = jnp.repeat(row_firsts.reshape(-1), 2)
    row_parity = jnp.arange(row_modes.shape[0], dtype=jnp.int32) % 2
    row_table = fourier(row_modes, row_parity, all_lons)
    grid_vals = jnp.einsum(
        "jq,iqc->jic",
        row_table,
        lax.all_to_all(second, "row", split_axis=2, concat_axis=1, tiled=True),
        precision=lax.Precision.HIGHEST,
    )
    row_done = lax.all_to_all(grid_vals, "row", split_axis=0, concat_axis=2, tiled=True)
    pts_row = row_done.shape[0] * NLAT
    spectral = row_done.reshape(pts_row, NLAT, 2 * col_orders)
    own_modes = jnp.repeat(lax.dynamic_index_in_dim(col_firsts, col_place, 0, keepdims=False), 2)
    own_parity = jnp.arange(2 * col_orders, dtype=jnp.int32) % 2
    pts_col = NLAT * NLON // col_count
    longitudes = jnp.arange(pts_col * lax.axis_size("col") // NLAT, dtype=jnp.int32)
    table_part = fourier(own_modes, own_parity, longitudes)
    grid_vals = jnp.einsum("jk,pik->jip", table_part, spectral, precision=lax.Precision.HIGHEST)
    summed = lax.psum_scatter(
        grid_vals.reshape(pts_col * lax.axis_size("col"), pts_row),
        "col",
        scatter_dimension=0,
        tiled=True,
    )
    result = summed.T
    return result


def solution(mesh):
    in_specs = (P("row", "col"), P())
    out_specs = P("row", "col")
    fits = mesh.shape["row"] == 2 * CHIPS and mesh.shape["col"] == 4
    return jax.shard_map(
        chunked if fits else on_device, mesh=mesh, in_specs=in_specs, out_specs=out_specs, check_vma=False
    )
```

```python
import functools
import math

import jax
import jax.numpy as jnp
from jax import lax
from jax.experimental import pallas as pl
from jax.experimental.pallas import tpu as pltpu
from jax.sharding import PartitionSpec as P

LL = 128
NLON = 384
NLAT = 12

F32 = jnp.float32
BF16 = jnp.bfloat16
ROWS16 = 16
CHIPS = 4
CHUNKS = NLAT // CHIPS
PAIR = 2 * LL
KEYS = 4
STEP = 2 * PAIR
GROUP = 2


def split(x):
    high = x.astype(BF16)
    return high, (x - high.astype(F32)).astype(BF16)


def dot3(a, b, dims):
    dg = functools.partial(
        lax.dot_general, dimension_numbers=(dims, ((), ())), preferred_element_type=F32
    )
    return dg(a[0], b[0]) + (dg(a[0], b[1]) + dg(a[1], b[0]))


def turn4(xs):
    lane = lax.broadcasted_iota(jnp.int32, xs[0].shape, 1)
    left = lane < 64
    even = (lane // 32) % 2 == 0
    out = [None] * 4
    halves = []
    for u in range(2):
        a, b = xs[u], xs[u + 2]
        halves.append(
            (jnp.where(left, a, pltpu.roll(b, 64, 1)), jnp.where(left, pltpu.roll(a, 64, 1), b))
        )
    for h in range(2):
        a, b = halves[0][h], halves[1][h]
        out[2 * h] = jnp.where(even, a, pltpu.roll(b, 32, 1))
        out[2 * h + 1] = jnp.where(even, pltpu.roll(a, 96, 1), b)
    return out


def legendre_table(by_degree, by_order):
    shape = (ROWS16, LL)
    lat = lax.broadcasted_iota(jnp.int32, shape, 0).astype(F32)
    colatitude = (NLON // 4 - NLAT // 2 + lat + 0.5) * (math.pi / (NLON // 2))
    cosine, sine = jnp.cos(colatitude), jnp.sin(colatitude)
    lane = lax.broadcasted_iota(jnp.int32, shape, 1)
    orders = lane.astype(F32)
    growth = jnp.sqrt((2.0 * orders + 1.0) / jnp.maximum(2.0 * orders, 1.0))
    growth = jnp.where(lane == 1, math.sqrt(3.0), jnp.where(lane == 0, 1.0, growth))
    total = jnp.log(growth)
    shift = 1
    while shift < LL:
        total = total + jnp.where(lane >= shift, pltpu.roll(total, shift, 1), 0.0)
        shift *= 2
    sectoral = jnp.exp(total + orders * jnp.log(sine))
    m8 = lax.broadcasted_iota(jnp.int32, (8, LL), 1).astype(F32)
    r8 = lax.broadcasted_iota(jnp.int32, (8, LL), 0)

    def block(b, carry):
        before, earlier = carry
        degree = (r8 + b * 8).astype(F32)
        plus, minus = degree + m8, degree - m8
        alpha = jnp.sqrt(
            jnp.maximum((2.0 * degree - 1.0) * (2.0 * degree + 1.0), 0.0)
            / jnp.maximum(minus * plus, 1.0)
        )
        beta = jnp.sqrt(
            jnp.maximum((2.0 * degree + 1.0) * (plus - 1.0) * (minus - 1.0), 0.0)
            / jnp.maximum(minus * plus * (2.0 * degree - 3.0), 1.0)
        )
        for r in range(8):
            l = b * 8 + r
            general = alpha[r : r + 1] * cosine * before - beta[r : r + 1] * earlier
            current = jnp.where(lane < l, general, jnp.where(lane == l, sectoral, 0.0))
            by_degree[pl.ds(pl.multiple_of(l * ROWS16, ROWS16), ROWS16), :] = current
            before, earlier = current, before
        return before, earlier

    zeros = jnp.zeros(shape, F32)
    lax.fori_loop(0, LL // 8, block, (zeros, zeros))
    for i in range(NLAT):
        by_order[pl.ds(i, LL, stride=ROWS16), :] = by_degree[pl.ds(i, LL, stride=ROWS16), :].T


def pair_weights(by_order, first, arrange):
    second = jnp.where(first == 0, LL // 2, LL - first)
    at = lambda m: arrange(by_order[pl.ds(pl.multiple_of(m * ROWS16, ROWS16), ROWS16), :])
    va, vb = at(first), at(second)
    na, nb = LL - first, LL - second
    lane = lax.broadcasted_iota(jnp.int32, va.shape, 1)
    wrap = lambda s: lax.bitwise_and(s, LL - 1)
    sines = pltpu.roll(va, wrap(2 * na), 1)
    real = first > 0
    begin = wrap(2 * na)
    return (
        (pltpu.roll(va, wrap(na), 1), None),
        (
            jnp.where((lane >= na) & real, sines, 0.0),
            jnp.where((lane < na) & real, sines, 0.0),
        ),
        (None, pltpu.roll(vb, wrap(nb + begin), 1)),
        (None, pltpu.roll(vb, wrap(2 * nb + begin), 1)),
    )


def order_sums_kernel(row_pairs, col_pairs, steps, index, cov, *refs):
    first_out, later_outs = refs[0], refs[1 : 1 + CHIPS]
    (
        held, by_degree, by_order, row_w, row_wb, col_w, col_wb, even, odd, second, orders, sems, order_sem
    ) = refs[1 + CHIPS :]
    row_place, col_place = lax.axis_index("row"), lax.axis_index("col")
    chip = row_place // 2
    pairs = [row_place * row_pairs + p for p in range(row_pairs)]
    pairs += [col_place * col_pairs + p for p in range(col_pairs)]
    heads = [
        pltpu.make_async_copy(
            index.at[1:2, pl.ds(pl.multiple_of(p * PAIR, PAIR), LL)],
            orders.at[n : n + 1, :],
            order_sem.at[n],
        )
        for n, p in enumerate(pairs)
    ]
    for head in heads:
        head.start()
    copy = lambda s: pltpu.make_async_copy(
        cov.at[:, pl.ds(pl.multiple_of(s * STEP, STEP), STEP)], held.at[s], sems.at[s]
    )
    for s in range(steps):
        copy(s).start()
    legendre_table(by_degree, by_order)
    for head in heads:
        head.wait()
    row_w[...] = jnp.zeros_like(row_w)
    col_w[...] = jnp.zeros_like(col_w)

    def own_first(v):
        place = lax.broadcasted_iota(jnp.int32, v.shape, 0)
        for bit in (1, 2):
            up = pltpu.roll(v, ROWS16 - bit, 0)
            down = pltpu.roll(v, bit, 0)
            swapped = jnp.where(lax.bitwise_and(place, bit) == 0, up, down)
            v = jnp.where(lax.bitwise_and(chip, bit) == 0, v, swapped)
        return v

    for p in range(row_pairs):
        for k, sides in enumerate(pair_weights(by_order, orders[p, 0], own_first)):
            for h, v in enumerate(sides):
                if v is not None:
                    row_w[
                        p % GROUP * 2 + h, pl.ds(p * KEYS * NLAT + k, NLAT, stride=KEYS), :
                    ] = v[:NLAT]
    for h in range(2 * GROUP):
        row_wb[:, h * LL : (h + 1) * LL] = row_w[h].astype(BF16)
    for p in range(col_pairs):
        s, e = p // 2, p % 2
        for k, sides in enumerate(
            pair_weights(by_order, orders[row_pairs + p, 0], lambda v: v)
        ):
            for h, v in enumerate(sides):
                if v is not None:
                    col_w[
                        2 * e + h, pl.ds(s * LL + e * KEYS + k, NLAT, stride=2 * KEYS), :
                    ] = v[:NLAT]
    for s in range(steps):
        for h in range(4):
            high, low = split(col_w[h, s * LL : (s + 1) * LL, :].T)
            col_wb[s, h * LL : (h + 1) * LL, :LL] = high
            col_wb[s, h * LL : (h + 1) * LL, LL:] = low

    blocks = row_pairs // GROUP
    own = lambda q: slice(q * GROUP * PAIR, (q + 1) * GROUP * PAIR)

    def column_block(s, half, q):
        both = jnp.dot(held[s, own(q), :], col_wb[s], preferred_element_type=F32)
        high, low = split(both[:, :LL] + both[:, LL:])
        half[own(q), :LL] = high
        half[own(q), LL:] = low

    def row_block(half, q):
        rows = GROUP * KEYS * NLAT
        both = jnp.dot(
            row_wb[q * rows : (q + 1) * rows, :], half[own(q), :], preferred_element_type=F32
        )
        both = both[:, :LL] + both[:, LL:]
        for g in range(GROUP):
            for i in range(NLAT):
                row = (i * row_pairs + q * GROUP + g) * KEYS
                from_row = (g * NLAT + i) * KEYS
                second[row : row + KEYS, :] = both[from_row : from_row + KEYS]

    def store(s):
        part = row_pairs * KEYS * NLAT
        for t in range(CHUNKS):
            turned = second[t * LL : (t + 1) * LL, :].T
            for g in range(NLAT // 4):
                xs = [turned[8 * (4 * g + u) : 8 * (4 * g + u + 1)] for u in range(4)]
                for d, x in enumerate(turn4(xs)):
                    lanes = slice(g * LL, (g + 1) * LL)
                    if t == 0:
                        lanes = slice(d * part + g * LL, d * part + (g + 1) * LL)
                        first_out[pl.ds(pl.multiple_of(s * 8, 8), 8), lanes] = x
                    else:
                        row = (t - 1) * steps * 8 + s * 8
                        later_outs[d][pl.ds(pl.multiple_of(row, 8), 8), lanes] = x

    def both_sides(s, now, later):
        copy(s + 1).wait()
        for q in range(blocks):
            row_block(now, q)
        for q in range(blocks - 1):
            column_block(s + 1, later, q)
        store(s)
        column_block(s + 1, later, blocks - 1)

    def step(j, carry):
        both_sides(2 * j, even, odd)
        both_sides(2 * j + 1, odd, even)
        return carry

    copy(0).wait()
    for q in range(blocks):
        column_block(0, even, q)
    lax.fori_loop(0, steps // 2 - 1, step, 0)
    both_sides(steps - 2, even, odd)
    for q in range(blocks):
        row_block(odd, q)
    store(steps - 1)


def order_sums(covariance, coef_index):
    rows_dev, cols_dev = covariance.shape
    row_pairs, col_pairs, steps = rows_dev // PAIR, cols_dev // PAIR, cols_dev // STEP
    lanes, keys = NLAT * row_pairs * KEYS, col_pairs * KEYS
    later = jax.ShapeDtypeStruct(((CHUNKS - 1) * keys, lanes), F32)
    return pl.pallas_call(
        functools.partial(order_sums_kernel, row_pairs, col_pairs, steps),
        out_shape=[jax.ShapeDtypeStruct((keys, CHIPS * lanes), F32)] + [later] * CHIPS,
        in_specs=[pl.BlockSpec(memory_space=pl.ANY)] * 2,
        out_specs=[pl.BlockSpec(memory_space=pltpu.VMEM)] * (1 + CHIPS),
        scratch_shapes=[
            pltpu.VMEM((steps, rows_dev, STEP), BF16),
            pltpu.VMEM((LL * ROWS16, LL), F32),
            pltpu.VMEM((LL * ROWS16, LL), F32),
            pltpu.VMEM((2 * GROUP, lanes, LL), F32),
            pltpu.VMEM((lanes, GROUP * PAIR), BF16),
            pltpu.VMEM((STEP // LL, steps * LL, LL), F32),
            pltpu.VMEM((steps, STEP, 2 * LL), BF16),
            pltpu.VMEM((rows_dev, 2 * LL), BF16),
            pltpu.VMEM((rows_dev, 2 * LL), BF16),
            pltpu.VMEM((lanes, LL), F32),
            pltpu.SMEM((row_pairs + col_pairs, LL), jnp.int32),
            pltpu.SemaphoreType.DMA((steps,)),
            pltpu.SemaphoreType.DMA((row_pairs + col_pairs,)),
        ],
        compiler_params=pltpu.CompilerParams(vmem_limit_bytes=56 * 1024 * 1024),
        cost_estimate=pl.CostEstimate(
            flops=2 * lanes * rows_dev * cols_dev,
            bytes_accessed=2 * rows_dev * cols_dev,
            transcendentals=0,
        ),
        name="order_sums",
    )(coef_index, covariance)


def columns_kernel(own, near, outer, far, table, result, partial, rhs):
    for s, ref in enumerate((own, near, outer, far)):
        n = ref.shape[0]
        rhs[s * n : (s + 1) * n, :] = ref[...]
    both = dot3(split(table[...]), split(rhs[...]), ((1,), (0,)))
    n = result.shape[0]
    result[...] = both[:n]
    partial[...] = both[n:]


def columns(own, near, outer, far, table):
    n, lanes = table.shape[0] // 2, own.shape[1]
    out = jax.ShapeDtypeStruct((n, lanes), F32)
    return pl.pallas_call(
        columns_kernel,
        out_shape=[out, out],
        in_specs=[pl.BlockSpec(memory_space=pltpu.VMEM)] * 5,
        out_specs=[pl.BlockSpec(memory_space=pltpu.VMEM)] * 2,
        scratch_shapes=[pltpu.VMEM((4 * own.shape[0], lanes), F32)],
        compiler_params=pltpu.CompilerParams(vmem_limit_bytes=32 * 1024 * 1024),
        cost_estimate=pl.CostEstimate(
            flops=6 * table.size * lanes, bytes_accessed=16 * own.size, transcendentals=0
        ),
        name="columns",
    )(own, near, outer, far, table)


def rows_kernel(mine, other, table, *refs):
    outs, turned = refs[:CHIPS], refs[CHIPS]
    n, lanes = mine.shape
    part = lanes // CHIPS
    for c, ref in enumerate((mine, other)):
        for g in range(NLAT // 4):
            xs = [ref[:, d * part + g * LL : d * part + (g + 1) * LL] for d in range(CHIPS)]
            for u, y in enumerate(turn4(xs)):
                turned[c, pl.ds(4 * g + u, n, stride=NLAT), :] = y
    values = jnp.concatenate([turned[0], turned[1]], axis=1)
    grid = dot3(split(table[...]), split(values), ((1,), (1,)))
    m = table.shape[0] // CHIPS
    for d in range(CHIPS):
        outs[d][...] = grid[d * m : (d + 1) * m]


def rows(mine, other, table):
    n, lanes = mine.shape
    m = table.shape[0] // CHIPS
    out = jax.ShapeDtypeStruct((m, n * NLAT), F32)
    return pl.pallas_call(
        rows_kernel,
        out_shape=[out] * CHIPS,
        in_specs=[pl.BlockSpec(memory_space=pltpu.VMEM)] * 3,
        out_specs=[pl.BlockSpec(memory_space=pltpu.VMEM)] * CHIPS,
        scratch_shapes=[pltpu.VMEM((2, n * NLAT, LL), F32)],
        compiler_params=pltpu.CompilerParams(vmem_limit_bytes=32 * 1024 * 1024),
        cost_estimate=pl.CostEstimate(
            flops=6 * table.size * n * NLAT, bytes_accessed=16 * mine.size, transcendentals=0
        ),
        name="rows",
    )(mine, other, table)


def place_kernel(*refs):
    parts, out, held = refs[:-2], refs[-2], refs[-1]
    tiles = held.shape[0]
    chip = lax.axis_index("row") // 2
    for t in range(CHUNKS):
        for d in range(CHIPS):
            ref = parts[t * CHIPS + d]
            row = 4 * t + lax.bitwise_xor(chip, d)
            for h in range(tiles):
                held[h, pl.ds(row, ref.shape[0], stride=NLAT), :] = ref[:, h * LL : (h + 1) * LL]
    for h in range(tiles):
        out[:, h * LL : (h + 1) * LL] = held[h]


def place(parts):
    m, lanes = parts[0].shape
    return pl.pallas_call(
        place_kernel,
        out_shape=jax.ShapeDtypeStruct((m * NLAT, lanes), F32),
        in_specs=[pl.BlockSpec(memory_space=pltpu.VMEM)] * len(parts),
        out_specs=pl.BlockSpec(memory_space=pltpu.VMEM),
        scratch_shapes=[pltpu.VMEM((lanes // LL, m * NLAT, LL), F32)],
        compiler_params=pltpu.CompilerParams(vmem_limit_bytes=32 * 1024 * 1024),
        name="place",
    )(*parts)


def wave(lons, keys):
    turns = (lons[:, None] * (keys // 2)[None, :] + (NLON // 4) * (1 - keys % 2)[None, :]) % NLON
    return jnp.sin(turns.astype(F32) * (2.0 * math.pi / NLON))


def tables(orders):
    row_place, col_place = lax.axis_index("row"), lax.axis_index("col")
    row_count, col_count = lax.axis_size("row"), lax.axis_size("col")
    second = jnp.where(orders == 0, LL // 2, LL - orders)
    keys = jnp.stack([2 * orders, 2 * orders + 1, 2 * second, 2 * second + 1], 1).reshape(-1)
    by_col = keys.reshape(col_count, -1)
    pick = lambda table, index: lax.dynamic_index_in_dim(table, index, 0, keepdims=False)
    col_keys = jnp.concatenate([pick(by_col, col_place ^ s) for s in (0, 3, 1, 2)])
    lons = jnp.arange(NLON // col_count, dtype=jnp.int32)
    col_lons = jnp.concatenate([lons + (col_place ^ s) * lons.size for s in (0, 1)])
    col_table = wave(col_lons, col_keys)
    n = by_col.shape[1]
    hidden = (jnp.arange(2 * lons.size) >= lons.size)[:, None] & (
        (jnp.arange(4 * n) // n) == 2
    )[None, :]
    col_table = jnp.where(hidden, 0.0, col_table)
    by_row = keys.reshape(row_count, -1)
    row_keys = jnp.concatenate(
        [pick(by_row, row_place ^ (2 * d + c)) for c in range(2) for d in range(CHIPS)]
    )
    lons = jnp.arange(NLON // row_count, dtype=jnp.int32)
    row_lons = jnp.concatenate(
        [lons + (row_place ^ (2 * d)) * lons.size for d in range(CHIPS)]
    )
    return col_table, wave(row_lons, row_keys)


def after(x, *done):
    return lax.optimization_barrier((x, *done))[0]


def chunked(covariance, coef_index):
    flip = lambda x, bits: lax.ppermute(
        x, "row", [(r, r ^ bits) for r in range(lax.axis_size("row"))]
    )
    along = lambda x, *pairs: lax.ppermute(x, "col", pairs)

    def spread(xs):
        return [xs[0]] + [flip(xs[d], 2 * d) for d in range(1, CHIPS)]

    def inward(own):
        outer = along(own, (0, 1), (3, 2))
        return along(own, (1, 2), (2, 1)), outer

    def across(outer):
        return along(outer, (1, 2), (2, 1))

    def outward(result, partial):
        return result + along(partial, (1, 0), (2, 3))

    def finish(result):
        return spread(rows(result, flip(result, 1), row_table))

    own0, *later = order_sums(covariance, coef_index)
    orders = after(coef_index, own0)[1].reshape(-1, PAIR)[:, 0]
    col_table, row_table = tables(orders)
    near0, outer0 = inward(own0)
    later = spread(later)
    far0 = across(outer0)
    keys = own0.shape[0]
    own1, own2 = (
        jnp.concatenate([x[t * keys : (t + 1) * keys] for x in later], axis=1) for t in range(2)
    )
    near1, outer1 = inward(after(own1, near0, outer0))
    result0, partial0 = columns(own0, near0, outer0, far0, col_table)
    far1 = across(after(outer1, far0))
    near2 = along(after(own2, near1, partial0), (1, 2), (2, 1))
    outer2 = along(after(own2, outer1, partial0), (0, 1), (3, 2))
    result0 = outward(result0, partial0)
    result1, partial1 = columns(own1, near1, outer1, far1, col_table)
    far2 = across(after(outer2, result0, partial1))
    lanes = result0.shape[1] // CHIPS
    result0 = jnp.concatenate(
        spread([result0[:, d * lanes : (d + 1) * lanes] for d in range(CHIPS)]), axis=1
    )
    result2, partial2 = columns(own2, near2, outer2, far2, after(col_table, result0))
    result1 = outward(result1, partial1)
    grid0 = finish(result0)
    result2 = outward(result2, after(partial2, result1))
    grid1 = finish(result1)
    grid2 = finish(after(result2, *grid0))
    return place(grid0 + grid1 + grid2)


def legendre_rows(lat_count, lon_count, degree_count):
    grid_rows = lon_count // 2
    first_row = grid_rows // 2 - lat_count // 2
    colatitude = (first_row + jnp.arange(lat_count, dtype=jnp.float32) + 0.5) * (
        math.pi / grid_rows
    )
    cosine = jnp.cos(colatitude)[:, None]
    sine_vals = jnp.sin(colatitude)[:, None]
    orders = jnp.arange(degree_count, dtype=jnp.float32)[None, :]
    growth = jnp.sqrt((2.0 * orders + 1.0) / jnp.maximum(2.0 * orders, 1.0))
    growth = jnp.where(
        orders == 1.0, jnp.sqrt(jnp.float32(3.0)), jnp.where(orders == 0.0, 1.0, growth)
    )
    sectoral = jnp.exp(jnp.cumsum(jnp.log(growth), axis=1) + orders * jnp.log(sine_vals))

    def advance(state_pair, degree):
        before, earlier = state_pair
        deg_sum = degree + orders
        deg_diff = degree - orders
        alpha_lm = jnp.sqrt(
            jnp.maximum((2.0 * degree - 1.0) * (2.0 * degree + 1.0), 0.0)
            / jnp.maximum(deg_diff * deg_sum, 1.0)
        )
        beta_lm = jnp.sqrt(
            jnp.maximum((2.0 * degree + 1.0) * (deg_sum - 1.0) * (deg_diff - 1.0), 0.0)
            / jnp.maximum(deg_diff * deg_sum * (2.0 * degree - 3.0), 1.0)
        )
        general = alpha_lm * cosine * before - beta_lm * earlier
        current = jnp.where(orders < degree, general, jnp.where(orders == degree, sectoral, 0.0))
        return ((current, before), current)

    start_pair = (
        jnp.zeros((lat_count, degree_count), jnp.float32),
        jnp.zeros((lat_count, degree_count), jnp.float32),
    )
    _, stacked = lax.scan(
        advance, start_pair, jnp.arange(degree_count, dtype=jnp.float32), unroll=16
    )
    return jnp.transpose(stacked, (1, 0, 2)).reshape(lat_count, degree_count * degree_count)


def fourier(modes, parity, longitudes):
    phases = longitudes[:, None] * modes[None, :] % NLON
    angles = phases.astype(jnp.float32) * (2.0 * math.pi / NLON)
    return jnp.where(parity[None, :] == 0, jnp.cos(angles), jnp.sin(angles))


def block_slots(orders_flat, blocks, length, slot_count):
    grouped = orders_flat.reshape(blocks, length)
    change = jnp.concatenate(
        [jnp.ones((blocks, 1), jnp.int32), (grouped[:, 1:] != grouped[:, :-1]).astype(jnp.int32)],
        axis=1,
    )
    slot_ids = jnp.cumsum(change, axis=1) - 1
    first_marks = (
        slot_ids[:, :, None] == jnp.arange(slot_count, dtype=jnp.int32)[None, None, :]
    ) & (change[:, :, None] == 1)
    firsts = jnp.sum(jnp.where(first_marks, grouped[:, :, None], 0), axis=1)
    return (slot_ids, firsts)


def spectral_weights(plm_table, degree, orders, parity, slot_ids, slot_count):
    values = plm_table[:, degree * LL + orders]
    key_ids = 2 * slot_ids + parity
    matches = key_ids[None, None, :] == jnp.arange(2 * slot_count, dtype=jnp.int32)[None, :, None]
    return jnp.where(matches, values[:, None, :], 0.0)


def on_device(covariance, coef_index):
    rows_dev, cols_dev = covariance.shape
    row_count = lax.axis_size("row")
    col_count = lax.axis_size("col")
    row_place = lax.axis_index("row")
    col_place = lax.axis_index("col")
    row_orders = max(LL // row_count, 2)
    col_orders = max(LL // col_count, 2)
    plm_table = legendre_rows(NLAT, NLON, LL)
    row_slots, row_firsts = block_slots(coef_index[1], row_count, rows_dev, row_orders)
    col_slots, col_firsts = block_slots(coef_index[1], col_count, cols_dev, col_orders)
    mine_rows = lax.dynamic_slice_in_dim(coef_index, row_place * rows_dev, rows_dev, 1)
    mine_cols = lax.dynamic_slice_in_dim(coef_index, col_place * cols_dev, cols_dev, 1)
    own_row_slots = lax.dynamic_index_in_dim(row_slots, row_place, 0, keepdims=False)
    own_col_slots = lax.dynamic_index_in_dim(col_slots, col_place, 0, keepdims=False)
    row_weights = spectral_weights(
        plm_table, mine_rows[0], mine_rows[1], mine_rows[2], own_row_slots, row_orders
    )
    row_weights = row_weights.astype(jnp.bfloat16).reshape(NLAT * 2 * row_orders, rows_dev)
    col_weights = spectral_weights(
        plm_table, mine_cols[0], mine_cols[1], mine_cols[2], own_col_slots, col_orders
    )
    first_pass = jnp.dot(row_weights, covariance, preferred_element_type=jnp.float32)
    second = jnp.einsum("ak,jbk->ajb", first_pass, col_weights, precision=lax.Precision.HIGHEST)
    width_cols = NLAT * 2 * col_orders
    second = second.reshape(NLAT, 2 * row_orders, width_cols)
    all_lons = jnp.arange(NLON, dtype=jnp.int32)
    row_modes = jnp.repeat(row_firsts.reshape(-1), 2)
    row_parity = jnp.arange(row_modes.shape[0], dtype=jnp.int32) % 2
    row_table = fourier(row_modes, row_parity, all_lons)
    grid_vals = jnp.einsum(
        "jq,iqc->jic",
        row_table,
        lax.all_to_all(second, "row", split_axis=2, concat_axis=1, tiled=True),
        precision=lax.Precision.HIGHEST,
    )
    row_done = lax.all_to_all(grid_vals, "row", split_axis=0, concat_axis=2, tiled=True)
    pts_row = row_done.shape[0] * NLAT
    spectral = row_done.reshape(pts_row, NLAT, 2 * col_orders)
    own_modes = jnp.repeat(lax.dynamic_index_in_dim(col_firsts, col_place, 0, keepdims=False), 2)
    own_parity = jnp.arange(2 * col_orders, dtype=jnp.int32) % 2
    pts_col = NLAT * NLON // col_count
    longitudes = jnp.arange(pts_col * lax.axis_size("col") // NLAT, dtype=jnp.int32)
    table_part = fourier(own_modes, own_parity, longitudes)
    grid_vals = jnp.einsum("jk,pik->jip", table_part, spectral, precision=lax.Precision.HIGHEST)
    summed = lax.psum_scatter(
        grid_vals.reshape(pts_col * lax.axis_size("col"), pts_row),
        "col",
        scatter_dimension=0,
        tiled=True,
    )
    result = summed.T
    return result


def solution(mesh):
    in_specs = (P("row", "col"), P())
    out_specs = P("row", "col")
    fits = mesh.shape["row"] == 2 * CHIPS and mesh.shape["col"] == 4
    return jax.shard_map(
        chunked if fits else on_device, mesh=mesh, in_specs=in_specs, out_specs=out_specs, check_vma=False
    )
```
